128 devices in a mesh: dp: 16 (over y, x), expert: 8 (over z, core).
Axes of the slice: x: 4, y: 4, z: 4, core: 2. Of those that a mesh axis runs over, the one named last changes fastest.
Arguments:
- tokens: bfloat16 [16384, 4096], P(('dp', 'expert')), may hold values from -6 to 6
- expert_ids: int32 [16384, 8], P(('dp', 'expert')), may hold values from 0 to 127, all different within a row; in each aligned block of 128 rows (0 to 127, 128 to 255, ...) at most 16 rows name the same one
- gates: float32 [16384, 8], P(('dp', 'expert')), may hold values from 0.1 to 1
- cotangent: bfloat16 [16384, 4096], P(('dp', 'expert')), may hold values from -6 to 6
- w_gate: bfloat16 [8, 4096, 768], P('expert', 'dp'), may hold values from -0.09375 to 0.09375
- w_up: bfloat16 [8, 4096, 768], P('expert', 'dp'), may hold values from -0.09375 to 0.09375
- w_down: bfloat16 [8, 4096, 768], P('expert', 'dp'), may hold values from -0.21875 to 0.21875
Outputs:
- mixed: bfloat16 [16384, 4096], P(('dp', 'expert'))
- grad_tokens: bfloat16 [16384, 4096], P(('dp', 'expert'))
- grad_gates: float32 [16384, 8], P(('dp', 'expert'))
- grad_w_gate: float32 [8, 4096, 768], P('expert', 'dp')
- grad_w_up: float32 [8, 4096, 768], P('expert', 'dp')
- grad_w_down: float32 [8, 4096, 768], P('expert', 'dp')
The draws below stay inside these ranges and needn't reach their ends.
Inputs may be any that keep to these rules, and one draw needn't show every extreme that they name: `expert_ids`: each token names 8 different experts; among the tokens of one device no expert is named more than 16 times.
All inputs are finite; a program needn't handle non-finite values.
Results may differ from the reference program's by a relative error of at most 0.015.
Values may be sent and summed in bfloat16 or wider, within the bound.
No kernel may reach another device: no remote copies, remote signals or barrier semaphores. Data moves between devices by JAX's collectives and lax.ppermute only.
A program may use at most 128 MiB of HBM per device.

```python
import math
import jax
import jax.numpy as jnp
import numpy as np
from jax import lax

D = 4096
EXPERTS = 128
TOPK = 8
FW = 768
TOK_DEV = 128
CAP = 16
EXP_WIN = 8
TOKENS = 16384
N_DP = 16
N_EXPERT = 8


def block_levels(key, shape, split, low, largest):
    gain = 1.0
    for position, parts in split:
        steps = jax.random.uniform(jax.random.fold_in(jax.random.fold_in(key, 6), position), (parts,), jnp.float32, low / len(split), largest / len(split))
        gain = gain * jnp.repeat(jnp.exp(steps), shape[position] // parts).reshape((-1,) + (1,) * (len(shape) - 1 - position))
    return gain


def shared_out(key, own, number, rows, count, top, reach, slope):
    ranking = jax.random.permutation(key, count)
    heavy_load, common = shares(count, rows * top, reach, slope, True), shares(count, rows * top, reach, slope, False)
    places = jnp.arange(count)

    def named(sizes, turn):
        used = int((sizes > 0).sum())
        fixed = max(1, used // 4)
        moved = fixed + (places - fixed + turn * (used - fixed)) % max(1, count - fixed)
        return jnp.zeros((count,), jnp.int32).at[ranking[jnp.where(places < fixed, places, moved)]].set(jnp.asarray(sizes, jnp.int32))

    sizes = jnp.where(number % 4 == 0, named(heavy_load, number // 4), named(common, number - number // 4 - 1))
    mixed = jax.random.permutation(jax.random.fold_in(own, 3), count)
    source_of, receiver = mixed[0:count // 2 * 2:2], mixed[1:count // 2 * 2:2]
    margin = jnp.minimum(sizes[source_of] - 1, reach - sizes[receiver]) // 2
    margin = jnp.where((source_of == ranking[0]) | (receiver == ranking[0]) | (sizes[receiver] == 0), 0, jnp.maximum(margin, 0))
    moved = jax.random.randint(jax.random.fold_in(own, 4), (count // 2,), 0, 1 << 20) % (margin + 1)
    sizes = sizes.at[source_of].add(-moved).at[receiver].add(moved)
    items = jnp.searchsorted(jnp.cumsum(sizes), jnp.arange(rows * top), side="right").astype(jnp.int32)
    listing = items.reshape(top, rows).T
    listing = listing[jax.random.permutation(jax.random.fold_in(own, 1), rows)]
    turn = jax.random.randint(jax.random.fold_in(own, 2), (rows, 1), 0, top)
    return jnp.take_along_axis(listing, (jnp.arange(top)[None, :] + turn) % top, axis=1)


def shares(number_of, total, bound, slope, full):
    weights = [(1 << 20) // math.isqrt(rank ** slope) + 1 for rank in range(1, number_of + 1)]
    largest = bound if full else min(bound, max(-(-total // number_of), total * weights[0] // sum(weights)))
    least = 1 if total - largest >= number_of - 1 else 0
    counts, surplus = [largest] + [least] * (number_of - 1), total - largest - least * (number_of - 1)
    while surplus > 0:
        free = [i for i in range(1, number_of) if counts[i] < largest] or [i for i in range(1, number_of) if counts[i] < bound]
        whole, left = sum([weights[i] for i in free]), surplus
        for i in free:
            more = min(bound - counts[i], max(1, left * weights[i] // whole), surplus)
            counts[i] = counts[i] + more
            surplus = surplus - more
    return np.array(counts)


def bell_draw(key, extent, width, reach, shards=(), kind=jnp.bfloat16):
    factor_of = block_levels(key, extent, shards, -0.22, 0.18) if shards else 1.0
    array = jax.random.normal(key, extent, jnp.float32) * width * factor_of
    return jnp.minimum(jnp.maximum(array, -reach), reach).astype(kind)


def setup_inputs(seed: int = 0) -> dict:
    arg_keys = jax.random.split(jax.random.key(seed), 8)
    tokens = bell_draw(arg_keys[0], (TOKENS, D), 1.0, 6.0, ((0, 128),))
    expert_ids_keys = jax.random.split(jax.random.fold_in(arg_keys[1], 1), TOKENS // TOK_DEV)
    expert_ids_turns = jax.random.permutation(jax.random.fold_in(arg_keys[1], 3), TOKENS // TOK_DEV)
    expert_ids = jax.vmap(lambda own, number: shared_out(jax.random.fold_in(arg_keys[1], 2), own, number, TOK_DEV, EXPERTS, TOPK, CAP, 2))(expert_ids_keys, expert_ids_turns).reshape((TOKENS, TOPK))
    gates = jnp.clip(0.1 + 0.9 * jax.random.uniform(arg_keys[2], (TOKENS, TOPK), jnp.float32) ** block_levels(arg_keys[2], (TOKENS, TOPK), ((0, 128),), -0.2, 0.2), 0.1, 1.0)
    cotangent = bell_draw(arg_keys[3], (TOKENS, D), 1.0, 6.0, ((0, 128),))
    w_gate = bell_draw(arg_keys[4], (EXP_WIN, D, FW), D ** -0.5, 0.09375, ((0, 8), (1, 16)))
    w_up = bell_draw(arg_keys[5], (EXP_WIN, D, FW), D ** -0.5, 0.09375, ((0, 8), (1, 16)))
    w_down = bell_draw(arg_keys[6], (EXP_WIN, D, FW), FW ** -0.5, 0.21875, ((0, 8), (1, 16)))
    return dict(tokens=tokens, expert_ids=expert_ids, gates=gates, cotangent=cotangent, w_gate=w_gate, w_up=w_up, w_down=w_down)


def rounded(value):
    return lax.optimization_barrier(value.astype(jnp.bfloat16)).astype(jnp.float32)


def reference(tokens, expert_ids, gates, cotangent, w_gate, w_up, w_down):
    groups = N_DP
    per = TOK_DEV * N_EXPERT
    slots = N_EXPERT * CAP
    x_all = tokens.reshape(groups, per, D)
    ids_all = expert_ids.reshape(groups, per, TOPK)
    gate_all = gates.reshape(groups, per, TOPK)
    dy_all = cotangent.reshape(groups, per, D)

    def one_group(totals, pieces):
        xg, idg, gg, dyg = pieces
        sum_gate, sum_up, sum_down = totals
        mixed = jnp.zeros((per, D), jnp.float32)
        d_tokens = jnp.zeros((per, D), jnp.float32)
        d_gates = jnp.zeros((per, TOPK), jnp.float32)
        for expert in range(EXP_WIN):
            hit = idg == expert
            used = jnp.any(hit, axis=1)
            gval = jnp.sum(jnp.where(hit, gg, jnp.float32(0.0)), axis=1)
            index = jnp.nonzero(used, size=slots, fill_value=0)[0].astype(jnp.int32)
            live = jnp.arange(slots, dtype=jnp.int32) < jnp.sum(used.astype(jnp.int32))
            rows = jnp.where(live[:, None], xg[index], jnp.zeros((), jnp.bfloat16))
            weight = jnp.where(live, gval[index], jnp.float32(0.0))
            dy_rows = dyg[index].astype(jnp.float32)
            wg = w_gate[expert]
            wu = w_up[expert]
            wd = w_down[expert]
            gate_pre = jnp.dot(rows, wg, preferred_element_type=jnp.float32)
            up_pre = jnp.dot(rows, wu, preferred_element_type=jnp.float32)
            sig = jax.nn.sigmoid(gate_pre)
            act = gate_pre * sig
            hidden = (act * up_pre).astype(jnp.bfloat16)
            produced = jnp.dot(hidden, wd.T, preferred_element_type=jnp.float32).astype(jnp.bfloat16)
            prod_f = produced.astype(jnp.float32)
            mixed = mixed.at[index].add(weight[:, None] * prod_f)
            score = jnp.sum(dy_rows * prod_f, axis=1) * live.astype(jnp.float32)
            token_score = jnp.zeros((per,), jnp.float32).at[index].add(score)
            d_gates = d_gates + jnp.where(hit, token_score[:, None], jnp.float32(0.0))
            grad_out = (weight[:, None] * dy_rows).astype(jnp.bfloat16)
            grad_hidden = jnp.dot(grad_out, wd, preferred_element_type=jnp.float32)
            grad_gate_pre = (grad_hidden * up_pre * sig * (1.0 + gate_pre * (1.0 - sig))).astype(jnp.bfloat16)
            grad_up_pre = (grad_hidden * act).astype(jnp.bfloat16)
            grad_rows = (jnp.dot(grad_gate_pre, wg.T, preferred_element_type=jnp.float32)
                         + jnp.dot(grad_up_pre, wu.T, preferred_element_type=jnp.float32)).astype(jnp.bfloat16)
            d_tokens = d_tokens.at[index].add(grad_rows.astype(jnp.float32) * live[:, None].astype(jnp.float32))
            part_gate = jnp.dot(rows.T, grad_gate_pre, preferred_element_type=jnp.float32)
            part_up = jnp.dot(rows.T, grad_up_pre, preferred_element_type=jnp.float32)
            part_down = jnp.dot(grad_out.T, hidden, preferred_element_type=jnp.float32)
            sum_gate = sum_gate.at[expert].add(rounded(part_gate))
            sum_up = sum_up.at[expert].add(rounded(part_up))
            sum_down = sum_down.at[expert].add(rounded(part_down))
        return (sum_gate, sum_up, sum_down), (mixed, d_tokens, d_gates)

    start = jnp.zeros((EXP_WIN, D, FW), jnp.float32)
    totals, outs = lax.scan(one_group, (start, start, start), (x_all, ids_all, gate_all, dy_all))
    mixed, d_tokens, d_gates = outs
    return (mixed.reshape(TOKENS, D).astype(jnp.bfloat16),
            d_tokens.reshape(TOKENS, D).astype(jnp.bfloat16),
            d_gates.reshape(TOKENS, TOPK),
            totals[0], totals[1], totals[2])
```

```python
import jax
import jax.numpy as jnp
from jax import lax
from jax.experimental import pallas as pl
from jax.experimental.pallas import tpu as pltpu
from jax.sharding import PartitionSpec as P

CAP = 16
SIDE = 4
AXES = ("dp", "expert")
BF = jnp.bfloat16
F32 = jnp.float32
REL = 8
COLS = 256
FW = 768
VMEM = 56 * 2**20


def _dev(y, x, z, c):
    return ((y % SIDE) * SIDE + x % SIDE) * 8 + (z % SIDE) * 2 + c % 2


def _perm(move):
    pairs = []
    for i in range(128):
        y, x, z, c = i // 32, i // 8 % 4, i // 2 % 4, i % 2
        pairs.append((i, _dev(*move(y, x, z, c))))
    return pairs


def shift_a(v, s):
    return lax.ppermute(
        v, AXES, _perm(lambda y, x, z, c: (y, x + s, z, c) if c == 0 else (y + s, x, z, c))
    )


def shift_b(v, s):
    return lax.ppermute(
        v, AXES, _perm(lambda y, x, z, c: (y + s, x, z, c) if c == 0 else (y, x + s, z, c))
    )


def shift_z(v, dz, dc):
    return lax.ppermute(v, AXES, _perm(lambda y, x, z, c: (y, x, z + dz, c + dc)))


def dot(left, right):
    return jnp.dot(left, right, preferred_element_type=F32)


def dot_last(left, right):
    return lax.dot_general(left, right, (((1,), (1,)), ((), ())), preferred_element_type=F32)


def dot_first(left, right):
    return lax.dot_general(left, right, (((0,), (0,)), ((), ())), preferred_element_type=F32)


def call(kernel, outs, ins, flops, smem=0):
    vm = pl.BlockSpec(memory_space=pltpu.VMEM)
    sm = pl.BlockSpec(memory_space=pltpu.SMEM)
    moved = sum(v.size * v.dtype.itemsize for v in list(ins[smem:]) + list(outs))
    return pl.pallas_call(
        kernel,
        out_shape=tuple(outs),
        in_specs=[sm] * smem + [vm] * (len(ins) - smem),
        out_specs=tuple([vm] * len(outs)),
        compiler_params=pltpu.CompilerParams(vmem_limit_bytes=VMEM),
        cost_estimate=pl.CostEstimate(flops=flops, bytes_accessed=moved, transcendentals=0),
    )(*ins)


def shape(dims, dtype=BF):
    return jax.ShapeDtypeStruct(dims, dtype)


def routing(place, ids, gates):
    tok = ids.shape[1]
    z, c = place[2], place[3]
    labels, used, weight = [], [], []
    for r in range(REL):
        label = ((z + r % 4) & 3) * 2 + (c ^ (r // 4))
        hit = ids == label
        labels.append(label)
        used.append(jnp.sum(jnp.where(hit, 1.0, 0.0), axis=0, keepdims=True))
        weight.append(jnp.sum(jnp.where(hit, gates, 0.0), axis=0, keepdims=True))
    used_all = jnp.concatenate(used, axis=0)
    before = lax.broadcasted_iota(jnp.int32, (tok, tok), 0) < lax.broadcasted_iota(
        jnp.int32, (tok, tok), 1
    )
    position = dot(used_all.astype(BF), jnp.where(before, 1.0, 0.0).astype(BF))
    slot = lax.broadcasted_iota(jnp.int32, (CAP, tok), 0).astype(F32)
    chosen, scale = [], []
    for r in range(REL):
        mask = (position[r : r + 1] == slot) & (used[r] > 0.5)
        chosen.append(jnp.where(mask, 1.0, 0.0))
        scale.append(jnp.sum(jnp.where(mask, weight[r], 0.0), axis=1, keepdims=True))
    return labels, jnp.concatenate(chosen, axis=0), jnp.concatenate(scale, axis=0)


def block_place(place, dc, yb, xb):
    y, x, c = place[0], place[1], place[3]
    dy, dx = (yb - y + 4) & 3, (xb - x + 4) & 3
    flip = c ^ dc
    sb = jnp.where(flip == 0, dy, dx)
    sa = (4 - jnp.where(flip == 0, dx, dy)) & 3
    return sb, sa


def dispatch_kernel(place, ids, gates, tokens, cotangent, *outs):
    _, chosen, scale = routing(place, ids[...], gates[...])
    chosen = chosen.astype(BF)
    for blk in range(16):
        cols = slice(blk * COLS, blk * COLS + COLS)
        rows = dot(chosen, tokens[:, cols]).astype(BF)
        grads = (scale * dot(chosen, cotangent[:, cols])).astype(BF)
        for dc in range(2):
            sb, sa = block_place(place, dc, blk // 4, blk % 4)
            lanes = pl.ds(pl.multiple_of(sa * COLS, COLS), COLS)
            for dz in range(4):
                r = dc * 4 + dz
                outs[r][0, sb, :, lanes] = rows[r * CAP : r * CAP + CAP]
                outs[r][1, sb, :, lanes] = grads[r * CAP : r * CAP + CAP]


def to_b_kernel(*refs):
    ins, outs = refs[:REL], refs[REL:]
    for s in range(SIDE):
        for r in range(REL):
            for kind in range(2):
                outs[s][kind, r * CAP : r * CAP + CAP, :] = ins[r][kind, s]


def to_z_kernel(*refs):
    ins, outs = refs[:SIDE], refs[SIDE:]
    for s in range(SIDE):
        for r in range(REL):
            for kind in range(2):
                outs[r][kind, s] = ins[s][kind, r * CAP : r * CAP + CAP, :]


def stacked(pieces, kind, cols=slice(None)):
    return jnp.concatenate([p[kind, :, cols] for p in pieces], axis=0)


def partial_kernel(*refs):
    xs, ws, own, outs = refs[:4], refs[4:8], refs[8], refs[9:]
    rows = xs[0].shape[1]
    for which in range(3):
        left = stacked(xs, 0 if which < 2 else 1)
        for n in range(FW // COLS):
            cols = slice(n * COLS, n * COLS + COLS)
            at = slice(which * FW + n * COLS, which * FW + n * COLS + COLS)
            got = dot(left, stacked(ws, which, cols))
            own[:, at] = got[:rows]
            for p in range(1, SIDE):
                outs[p - 1][:, at] = got[p * rows : p * rows + rows].astype(BF)


def hidden_kernel(own, p1, p2, p3, out):
    def full(which):
        at = slice(which * FW, which * FW + FW)
        return (own[:, at] + p1[:, at].astype(F32)) + (
            p2[:, at].astype(F32) + p3[:, at].astype(F32)
        )

    gate, up, grad = full(0), full(1), full(2)
    sig = jax.nn.sigmoid(gate)
    act = gate * sig
    out[:, :FW] = (act * up).astype(BF)
    out[:, FW : 2 * FW] = (grad * up * sig * (1.0 + gate * (1.0 - sig))).astype(BF)
    out[:, 2 * FW :] = (grad * act).astype(BF)


def rows_kernel(*refs):
    hs, ws, outs = refs[:4], refs[4:8], refs[8:]
    rows = hs[0].shape[0]
    hidden, ggate, gup = (
        jnp.concatenate([h[:, k * FW : k * FW + FW] for h in hs], axis=0) for k in range(3)
    )
    for a in range(SIDE):
        cols = slice(a * COLS, a * COLS + COLS)
        made = dot_last(hidden, ws[a][2]).astype(BF)
        back = (dot_last(ggate, ws[a][0]) + dot_last(gup, ws[a][1])).astype(BF)
        for p in range(SIDE):
            outs[p][0, :, cols] = made[p * rows : p * rows + rows]
            outs[p][1, :, cols] = back[p * rows : p * rows + rows]


def weights_kernel(*refs):
    hs, xs, own, outs = refs[:4], refs[4:8], refs[8], refs[9:]
    hidden, ggate, gup = (
        jnp.concatenate([h[:, k * FW : k * FW + FW] for h in hs], axis=0) for k in range(3)
    )
    for a in range(SIDE):
        cols = slice(a * COLS, a * COLS + COLS)
        x, g = stacked(xs, 0, cols), stacked(xs, 1, cols)
        for k, (left, right) in enumerate(((x, ggate), (x, gup), (g, hidden))):
            got = dot_first(left, right)
            if a == 0:
                own[k] = got
            else:
                outs[a - 1][k] = got.astype(BF)


def total_kernel(own, p1, p2, p3, *outs):
    for k in range(3):
        outs[k][0] = (own[k] + p1[k].astype(F32)) + (p2[k].astype(F32) + p3[k].astype(F32))


def combine_kernel(place, ids, gates, cotangent, *refs):
    backs, (mixed, gtok, ggates) = refs[:REL], refs[REL:]
    labels, chosen, scale = routing(place, ids[...], gates[...])
    spread = chosen.T.astype(BF)
    scores = jnp.zeros(chosen.shape, F32)
    for blk in range(16):
        cols = slice(blk * COLS, blk * COLS + COLS)
        made, grads = [], []
        for dc in range(2):
            sb, sa = block_place(place, dc, blk // 4, blk % 4)
            lanes = pl.ds(pl.multiple_of(sa * COLS, COLS), COLS)
            for dz in range(4):
                made.append(backs[dc * 4 + dz][0, sb, :, lanes])
                grads.append(backs[dc * 4 + dz][1, sb, :, lanes])
        made, grads = jnp.concatenate(made, axis=0), jnp.concatenate(grads, axis=0)
        scaled = scale * made.astype(F32)
        upper = scaled.astype(BF)
        lower = (scaled - upper.astype(F32)).astype(BF)
        mixed[:, cols] = (dot(spread, upper) + dot(spread, lower)).astype(BF)
        gtok[:, cols] = dot(spread, grads).astype(BF)
        scores += dot_last(made, cotangent[:, cols])
    picked = chosen * scores
    total = jnp.zeros(ids.shape, F32)
    for r in range(REL):
        mine = jnp.sum(picked[r * CAP : r * CAP + CAP], axis=0, keepdims=True)
        total += jnp.where(ids[...] == labels[r], mine, 0.0)
    ggates[...] = total


def per_device(tokens, expert_ids, gates, cotangent, w_gate, w_up, w_down):
    tok, width = tokens.shape
    dp, ex = lax.axis_index("dp"), lax.axis_index("expert")
    place = jnp.stack([dp // 4, dp % 4, ex // 2, ex % 2]).astype(jnp.int32)
    ids_t, gates_t = expert_ids.T, gates.T
    chunk = width // SIDE

    held = jnp.concatenate([w_gate, w_up, w_down], axis=0)
    ws = [held] + [shift_a(held, s) for s in (1, 2, 3)]

    sends = call(
        dispatch_kernel,
        [shape((2, SIDE, CAP, chunk))] * REL,
        (place, ids_t, gates_t, tokens, cotangent),
        4 * tok * tok * width,
        smem=1,
    )
    came = [sends[0]] + [shift_z(sends[r], r % 4, r // 4) for r in range(1, REL)]
    turned = call(to_b_kernel, [shape((2, REL * CAP, chunk))] * SIDE, came, 0)
    xs = [turned[0]] + [shift_b(turned[s], s) for s in (1, 2, 3)]

    rows = REL * CAP
    parts = call(
        partial_kernel,
        [shape((rows, 3 * FW), F32)] + [shape((rows, 3 * FW))] * 3,
        (*xs, *ws),
        2 * SIDE * rows * chunk * 3 * FW,
    )
    others = [shift_b(parts[s], -s) for s in (1, 2, 3)]
    (mid,) = call(hidden_kernel, [shape((rows, 3 * FW))], (parts[0], *others), 0)
    hs = [mid] + [shift_b(mid, s) for s in (1, 2, 3)]

    outs = call(
        rows_kernel,
        [shape((2, rows, chunk))] * SIDE,
        (*hs, *ws),
        2 * SIDE * rows * chunk * 3 * FW,
    )
    home = [outs[0]] + [shift_b(outs[s], -s) for s in (1, 2, 3)]
    grads = call(
        weights_kernel,
        [shape((3, COLS, FW), F32)] + [shape((3, COLS, FW))] * 3,
        (*hs, *xs),
        2 * SIDE * rows * chunk * 3 * FW,
    )
    others_w = [shift_a(grads[s], -s) for s in (1, 2, 3)]
    split = call(to_z_kernel, [shape((2, SIDE, CAP, chunk))] * REL, home, 0)
    backs = [split[0]] + [shift_z(split[r], -(r % 4), r // 4) for r in range(1, REL)]
    gw = call(total_kernel, [shape((1, COLS, FW), F32)] * 3, (grads[0], *others_w), 0)
    mixed, gtok, gg_t = call(
        combine_kernel,
        [shape((tok, width)), shape((tok, width)), shape(ids_t.shape, F32)],
        (place, ids_t, gates_t, cotangent, *backs),
        8 * tok * tok * width,
        smem=1,
    )
    return mixed, gtok, gg_t.T, *gw


def solution(mesh):
    rows, cut = P(("dp", "expert"), None), P("expert", "dp", None)
    return jax.shard_map(
        per_device,
        mesh=mesh,
        in_specs=(rows,) * 4 + (cut,) * 3,
        out_specs=(rows,) * 3 + (cut,) * 3,
        check_vma=False,
    )
```

```python
import jax
import jax.numpy as jnp
from jax import lax
from jax.experimental import pallas as pl
from jax.experimental.pallas import tpu as pltpu
from jax.sharding import PartitionSpec as P

CAP = 16
SIDE = 4
AXES = ("dp", "expert")
BF = jnp.bfloat16
F32 = jnp.float32
REL = 8
COLS = 256
FW = 768
VMEM = 56 * 2**20


def _dev(y, x, z, c):
    return ((y % SIDE) * SIDE + x % SIDE) * 8 + (z % SIDE) * 2 + c % 2


def _perm(move):
    pairs = []
    for i in range(128):
        y, x, z, c = i // 32, i // 8 % 4, i // 2 % 4, i % 2
        pairs.append((i, _dev(*move(y, x, z, c))))
    return pairs


def groups_a():
    groups = [[_dev(y, x, z, 0) for x in range(4)] for y in range(4) for z in range(4)]
    return groups + [[_dev(y, x, z, 1) for y in range(4)] for x in range(4) for z in range(4)]


def shift_b(v, s):
    return lax.ppermute(
        v, AXES, _perm(lambda y, x, z, c: (y + s, x, z, c) if c == 0 else (y, x + s, z, c))
    )


def shift_z(v, dz, dc):
    return lax.ppermute(v, AXES, _perm(lambda y, x, z, c: (y, x, z + dz, c + dc)))


def dot(left, right):
    return jnp.dot(left, right, preferred_element_type=F32)


def dot_last(left, right):
    return lax.dot_general(left, right, (((1,), (1,)), ((), ())), preferred_element_type=F32)


def dot_first(left, right):
    return lax.dot_general(left, right, (((0,), (0,)), ((), ())), preferred_element_type=F32)


def call(kernel, outs, ins, flops, smem=0):
    vm = pl.BlockSpec(memory_space=pltpu.VMEM)
    sm = pl.BlockSpec(memory_space=pltpu.SMEM)
    moved = sum(v.size * v.dtype.itemsize for v in list(ins[smem:]) + list(outs))
    return pl.pallas_call(
        kernel,
        out_shape=tuple(outs),
        in_specs=[sm] * smem + [vm] * (len(ins) - smem),
        out_specs=tuple([vm] * len(outs)),
        compiler_params=pltpu.CompilerParams(vmem_limit_bytes=VMEM),
        cost_estimate=pl.CostEstimate(flops=flops, bytes_accessed=moved, transcendentals=0),
    )(*ins)


def shape(dims, dtype=BF):
    return jax.ShapeDtypeStruct(dims, dtype)


def routing(place, ids, gates):
    tok = ids.shape[1]
    z, c = place[2], place[3]
    labels, used, weight = [], [], []
    for r in range(REL):
        label = ((z + r % 4) & 3) * 2 + (c ^ (r // 4))
        hit = ids == label
        labels.append(label)
        used.append(jnp.sum(jnp.where(hit, 1.0, 0.0), axis=0, keepdims=True))
        weight.append(jnp.sum(jnp.where(hit, gates, 0.0), axis=0, keepdims=True))
    used_all = jnp.concatenate(used, axis=0)
    before = lax.broadcasted_iota(jnp.int32, (tok, tok), 0) < lax.broadcasted_iota(
        jnp.int32, (tok, tok), 1
    )
    position = dot(used_all.astype(BF), jnp.where(before, 1.0, 0.0).astype(BF))
    slot = lax.broadcasted_iota(jnp.int32, (CAP, tok), 0).astype(F32)
    chosen, scale = [], []
    for r in range(REL):
        mask = (position[r : r + 1] == slot) & (used[r] > 0.5)
        chosen.append(jnp.where(mask, 1.0, 0.0))
        scale.append(jnp.sum(jnp.where(mask, weight[r], 0.0), axis=1, keepdims=True))
    return labels, jnp.concatenate(chosen, axis=0), jnp.concatenate(scale, axis=0)


def block_place(place, dc, yb, xb):
    y, x, c = place[0], place[1], place[3]
    dy, dx = (yb - y + 4) & 3, (xb - x + 4) & 3
    flip = c ^ dc
    return jnp.where(flip == 0, dy, dx), jnp.where(flip == 0, xb, yb)


def dispatch_kernel(place, ids, gates, tokens, cotangent, *outs):
    _, chosen, scale = routing(place, ids[...], gates[...])
    chosen = chosen.astype(BF)
    for blk in range(16):
        cols = slice(blk * COLS, blk * COLS + COLS)
        rows = dot(chosen, tokens[:, cols]).astype(BF)
        grads = (scale * dot(chosen, cotangent[:, cols])).astype(BF)
        for dc in range(2):
            sb, sa = block_place(place, dc, blk // 4, blk % 4)
            lanes = pl.ds(pl.multiple_of(sa * COLS, COLS), COLS)
            for dz in range(4):
                r = dc * 4 + dz
                outs[r][0, sb, :, lanes] = rows[r * CAP : r * CAP + CAP]
                outs[r][1, sb, :, lanes] = grads[r * CAP : r * CAP + CAP]


def to_b_kernel(*refs):
    ins, outs = refs[:SIDE], refs[SIDE:]
    for s in range(SIDE):
        for r in range(SIDE):
            for kind in range(2):
                outs[s][kind, r * CAP : r * CAP + CAP, :] = ins[r][kind, s]


def to_z_kernel(*refs):
    ins, outs = refs[:SIDE], refs[SIDE:]
    for s in range(SIDE):
        for r in range(SIDE):
            for kind in range(2):
                outs[r][kind, s] = ins[s][kind, r * CAP : r * CAP + CAP, :]


def stacked(pieces, kind, cols=slice(None)):
    return jnp.concatenate([p[kind, :, cols] for p in pieces], axis=0)


def thirds(pieces):
    return [jnp.concatenate([p[:, k * FW : k * FW + FW] for p in pieces], axis=0) for k in range(3)]


def partial_kernel(*refs):
    xs, ws, own, outs = refs[:4], refs[4], refs[5], refs[6:]
    rows = xs[0].shape[1]
    for which in range(3):
        left = stacked(xs, 0 if which < 2 else 1)
        for n in range(FW // COLS):
            cols = slice(n * COLS, n * COLS + COLS)
            at = slice(which * FW + n * COLS, which * FW + n * COLS + COLS)
            right = jnp.concatenate([ws[a, which, :, cols] for a in range(SIDE)], axis=0)
            got = dot(left, right)
            own[:, at] = got[:rows]
            for p in range(1, SIDE):
                outs[p - 1][:, at] = got[p * rows : p * rows + rows].astype(BF)


def hidden_kernel(own, p1, p2, p3, out):
    def full(which):
        at = slice(which * FW, which * FW + FW)
        return (own[:, at] + p1[:, at].astype(F32)) + (
            p2[:, at].astype(F32) + p3[:, at].astype(F32)
        )

    gate, up, grad = full(0), full(1), full(2)
    sig = jax.nn.sigmoid(gate)
    act = gate * sig
    out[:, :FW] = (act * up).astype(BF)
    out[:, FW : 2 * FW] = (grad * up * sig * (1.0 + gate * (1.0 - sig))).astype(BF)
    out[:, 2 * FW :] = (grad * act).astype(BF)


def rows_kernel(*refs):
    hs, ws, outs = refs[:4], refs[4], refs[5:]
    rows = hs[0].shape[0]
    hidden, ggate, gup = thirds(hs)
    for a in range(SIDE):
        cols = slice(a * COLS, a * COLS + COLS)
        made = dot_last(hidden, ws[a, 2]).astype(BF)
        back = (dot_last(ggate, ws[a, 0]) + dot_last(gup, ws[a, 1])).astype(BF)
        for p in range(SIDE):
            outs[p][0, :, cols] = made[p * rows : p * rows + rows]
            outs[p][1, :, cols] = back[p * rows : p * rows + rows]


def weights_kernel(*refs):
    hs, xs, out = refs[:8], refs[8:16], refs[16]
    hidden, ggate, gup = thirds(hs)
    for a in range(SIDE):
        cols = slice(a * COLS, a * COLS + COLS)
        x, g = stacked(xs, 0, cols), stacked(xs, 1, cols)
        for k, (left, right) in enumerate(((x, ggate), (x, gup), (g, hidden))):
            out[a, k] = dot_first(left, right).astype(BF)


def combine_kernel(place, ids, gates, cotangent, *refs):
    backs, (mixed, gtok, ggates) = refs[:REL], refs[REL:]
    labels, chosen, scale = routing(place, ids[...], gates[...])
    spread = chosen.T.astype(BF)
    scores = jnp.zeros(chosen.shape, F32)
    for blk in range(16):
        cols = slice(blk * COLS, blk * COLS + COLS)
        made, grads = [], []
        for dc in range(2):
            sb, sa = block_place(place, dc, blk // 4, blk % 4)
            lanes = pl.ds(pl.multiple_of(sa * COLS, COLS), COLS)
            for dz in range(4):
                made.append(backs[dc * 4 + dz][0, sb, :, lanes])
                grads.append(backs[dc * 4 + dz][1, sb, :, lanes])
        made, grads = jnp.concatenate(made, axis=0), jnp.concatenate(grads, axis=0)
        scaled = scale * made.astype(F32)
        upper = scaled.astype(BF)
        lower = (scaled - upper.astype(F32)).astype(BF)
        mixed[:, cols] = (dot(spread, upper) + dot(spread, lower)).astype(BF)
        gtok[:, cols] = dot(spread, grads).astype(BF)
        scores += dot_last(made, cotangent[:, cols])
    picked = chosen * scores
    total = jnp.zeros(ids.shape, F32)
    for r in range(REL):
        mine = jnp.sum(picked[r * CAP : r * CAP + CAP], axis=0, keepdims=True)
        total += jnp.where(ids[...] == labels[r], mine, 0.0)
    ggates[...] = total


def per_device(tokens, expert_ids, gates, cotangent, w_gate, w_up, w_down):
    tok, width = tokens.shape
    dp, ex = lax.axis_index("dp"), lax.axis_index("expert")
    place = jnp.stack([dp // 4, dp % 4, ex // 2, ex % 2]).astype(jnp.int32)
    ids_t, gates_t = expert_ids.T, gates.T
    chunk = width // SIDE
    rows = SIDE * CAP
    work = 2 * SIDE * rows * chunk * 3 * FW

    held = jnp.concatenate([w_gate, w_up, w_down], axis=0)
    ws = lax.all_gather(held, AXES, axis_index_groups=groups_a())

    sends = call(
        dispatch_kernel,
        [shape((2, SIDE, CAP, chunk))] * REL,
        (place, ids_t, gates_t, tokens, cotangent),
        4 * tok * tok * width,
        smem=1,
    )
    came = [sends[0]] + [shift_z(sends[r], r % 4, r // 4) for r in range(1, REL)]
    xs, hs, backs = [], [], []
    for half in range(2):
        turned = call(
            to_b_kernel,
            [shape((2, rows, chunk))] * SIDE,
            came[half * SIDE : half * SIDE + SIDE],
            0,
        )
        xs.append([turned[0]] + [shift_b(turned[s], s) for s in (1, 2, 3)])
    for half in range(2):
        parts = call(
            partial_kernel,
            [shape((rows, 3 * FW), F32)] + [shape((rows, 3 * FW))] * 3,
            (*xs[half], ws),
            work,
        )
        others = [shift_b(parts[s], -s) for s in (1, 2, 3)]
        (mid,) = call(hidden_kernel, [shape((rows, 3 * FW))], (parts[0], *others), 0)
        hs.append([mid] + [shift_b(mid, s) for s in (1, 2, 3)])
    (grads,) = call(
        weights_kernel, [shape((SIDE, 3, COLS, FW))], (*hs[0], *hs[1], *xs[0], *xs[1]), 2 * work
    )
    total = lax.psum_scatter(grads, AXES, axis_index_groups=groups_a()).astype(F32)
    for half in range(2):
        outs = call(rows_kernel, [shape((2, rows, chunk))] * SIDE, (*hs[half], ws), work)
        home = [outs[0]] + [shift_b(outs[s], -s) for s in (1, 2, 3)]
        split = call(to_z_kernel, [shape((2, SIDE, CAP, chunk))] * SIDE, home, 0)
        backs += [
            split[dz] if dz + half == 0 else shift_z(split[dz], -dz, half) for dz in range(SIDE)
        ]
    mixed, gtok, gg_t = call(
        combine_kernel,
        [shape((tok, width)), shape((tok, width)), shape(ids_t.shape, F32)],
        (place, ids_t, gates_t, cotangent, *backs),
        8 * tok * tok * width,
        smem=1,
    )
    return mixed, gtok, gg_t.T, total[:1], total[1:2], total[2:]


def solution(mesh):
    rows, cut = P(("dp", "expert"), None), P("expert", "dp", None)
    return jax.shard_map(
        per_device,
        mesh=mesh,
        in_specs=(rows,) * 4 + (cut,) * 3,
        out_specs=(rows,) * 3 + (cut,) * 3,
        check_vma=False,
    )
```

```python
import jax
import jax.numpy as jnp
from jax import lax
from jax.experimental import pallas as pl
from jax.experimental.pallas import tpu as pltpu
from jax.sharding import PartitionSpec as P

CAP = 16
SIDE = 4
AXES = ("dp", "expert")
BF = jnp.bfloat16
F32 = jnp.float32
REL = 8
COLS = 256
FW = 768
VMEM = 12 * 2**20


def _dev(y, x, z, c):
    return ((y % SIDE) * SIDE + x % SIDE) * 8 + (z % SIDE) * 2 + c % 2


def _perm(move):
    pairs = []
    for i in range(128):
        y, x, z, c = i // 32, i // 8 % 4, i // 2 % 4, i % 2
        pairs.append((i, _dev(*move(y, x, z, c))))
    return pairs


def groups_a():
    groups = [[_dev(y, x, z, 0) for x in range(4)] for y in range(4) for z in range(4)]
    return groups + [[_dev(y, x, z, 1) for y in range(4)] for x in range(4) for z in range(4)]


def shift_b(v, s):
    return lax.ppermute(
        v, AXES, _perm(lambda y, x, z, c: (y + s, x, z, c) if c == 0 else (y, x + s, z, c))
    )


def shift_z(v, dz, dc):
    return lax.ppermute(v, AXES, _perm(lambda y, x, z, c: (y, x, z + dz, c + dc)))


def dot(left, right):
    return jnp.dot(left, right, preferred_element_type=F32)


def dot_last(left, right):
    return lax.dot_general(left, right, (((1,), (1,)), ((), ())), preferred_element_type=F32)


def dot_first(left, right):
    return lax.dot_general(left, right, (((0,), (0,)), ((), ())), preferred_element_type=F32)


def call(kernel, outs, ins, flops, smem=0, hbm=0, scratch=(), vmem=VMEM):
    spaces = [pltpu.SMEM] * smem + [pltpu.HBM] * hbm + [pltpu.VMEM] * (len(ins) - smem - hbm)
    return pl.pallas_call(
        kernel,
        out_shape=tuple(outs),
        in_specs=[pl.BlockSpec(memory_space=space) for space in spaces],
        out_specs=tuple(pl.BlockSpec(memory_space=pltpu.VMEM) for _ in outs),
        scratch_shapes=list(scratch),
        compiler_params=pltpu.CompilerParams(vmem_limit_bytes=vmem),
        cost_estimate=pl.CostEstimate(flops=flops // 100, bytes_accessed=1024, transcendentals=0),
    )(*ins)


def shape(dims, dtype=BF):
    return jax.ShapeDtypeStruct(dims, dtype)


def routing(place, ids, gates):
    tok = ids.shape[1]
    z, c = place[2], place[3]
    labels, used, weight = [], [], []
    for r in range(REL):
        label = ((z + r % 4) & 3) * 2 + (c ^ (r // 4))
        hit = ids == label
        labels.append(label)
        used.append(jnp.sum(jnp.where(hit, 1.0, 0.0), axis=0, keepdims=True))
        weight.append(jnp.sum(jnp.where(hit, gates, 0.0), axis=0, keepdims=True))
    used_all = jnp.concatenate(used, axis=0)
    before = lax.broadcasted_iota(jnp.int32, (tok, tok), 0) < lax.broadcasted_iota(
        jnp.int32, (tok, tok), 1
    )
    position = dot(used_all.astype(BF), jnp.where(before, 1.0, 0.0).astype(BF))
    slot = lax.broadcasted_iota(jnp.int32, (CAP, tok), 0).astype(F32)
    chosen, scale = [], []
    for r in range(REL):
        mask = (position[r : r + 1] == slot) & (used[r] > 0.5)
        chosen.append(jnp.where(mask, 1.0, 0.0))
        scale.append(jnp.sum(jnp.where(mask, weight[r], 0.0), axis=1, keepdims=True))
    return labels, jnp.concatenate(chosen, axis=0), jnp.concatenate(scale, axis=0)


def block_place(place, dc, yb, xb):
    y, x, c = place[0], place[1], place[3]
    dy, dx = (yb - y + 4) & 3, (xb - x + 4) & 3
    flip = c ^ dc
    return jnp.where(flip == 0, dy, dx), jnp.where(flip == 0, xb, yb)


def dispatch_kernel(place, ids, gates, tokens, cotangent, *refs):
    outs, (ids_v, gates_v, tok_v, cot_v, sem) = refs[:REL], refs[REL:]
    small = [
        pltpu.make_async_copy(ids, ids_v, sem.at[0]),
        pltpu.make_async_copy(gates, gates_v, sem.at[1]),
    ]
    wide, quarter = [], tokens.shape[1] // SIDE
    for q in range(SIDE):
        cols = slice(q * quarter, q * quarter + quarter)
        wide.append(
            (
                pltpu.make_async_copy(tokens.at[:, cols], tok_v.at[q], sem.at[2 + 2 * q]),
                pltpu.make_async_copy(cotangent.at[:, cols], cot_v.at[q], sem.at[3 + 2 * q]),
            )
        )
    for copy in small + [c for pair in wide for c in pair]:
        copy.start()
    for copy in small:
        copy.wait()
    _, chosen, scale = routing(place, ids_v[...], gates_v[...])
    chosen = chosen.astype(BF)
    for blk in range(16):
        q, cols = blk // 4, slice(blk % 4 * COLS, blk % 4 * COLS + COLS)
        if blk % 4 == 0:
            for copy in wide[q]:
                copy.wait()
        rows = dot(chosen, tok_v[q, :, cols]).astype(BF)
        grads = (scale * dot(chosen, cot_v[q, :, cols])).astype(BF)
        for dc in range(2):
            sb, sa = block_place(place, dc, blk // 4, blk % 4)
            lanes = pl.ds(pl.multiple_of(sa * COLS, COLS), COLS)
            for dz in range(4):
                r = dc * 4 + dz
                outs[r][0, sb, :, lanes] = rows[r * CAP : r * CAP + CAP]
                outs[r][1, sb, :, lanes] = grads[r * CAP : r * CAP + CAP]


def to_b_kernel(*refs):
    ins, outs = refs[:SIDE], refs[SIDE:]
    for s in range(SIDE):
        for r in range(SIDE):
            for kind in range(2):
                outs[s][kind, r * CAP : r * CAP + CAP, :] = ins[r][kind, s]


def to_z_kernel(*refs):
    ins, outs = refs[:SIDE], refs[SIDE:]
    for s in range(SIDE):
        for r in range(SIDE):
            for kind in range(2):
                outs[r][kind, s] = ins[s][kind, r * CAP : r * CAP + CAP, :]


def stacked(pieces, kind, cols=slice(None)):
    return jnp.concatenate([p[kind, :, cols] for p in pieces], axis=0)


def thirds(pieces):
    return [jnp.concatenate([p[:, k * FW : k * FW + FW] for p in pieces], axis=0) for k in range(3)]


def held_kernel(gate, up, down, out, sem):
    copies = [
        pltpu.make_async_copy(w.at[0], out.at[k], sem.at[k]) for k, w in enumerate((gate, up, down))
    ]
    for copy in copies:
        copy.start()
    for copy in copies:
        copy.wait()


def partial_kernel(*refs):
    xs, ws, outs = refs[:8], refs[8], refs[9:]
    rows = xs[0].shape[1]
    for which in range(3):
        left = stacked(xs, 0 if which < 2 else 1)
        for n in range(FW // COLS):
            cols = slice(n * COLS, n * COLS + COLS)
            at = slice(which * FW + n * COLS, which * FW + n * COLS + COLS)
            right = jnp.concatenate([ws[a, which, :, cols] for a in range(SIDE)], axis=0)
            got = dot(left, right)
            for p in range(2 * SIDE):
                outs[p][:, at] = got[p * rows : p * rows + rows].astype(outs[p].dtype)


def hidden_kernel(own, p1, p2, p3, out):
    def full(which):
        at = slice(which * FW, which * FW + FW)
        return (own[:, at] + p1[:, at].astype(F32)) + (
            p2[:, at].astype(F32) + p3[:, at].astype(F32)
        )

    gate, up, grad = full(0), full(1), full(2)
    sig = jax.nn.sigmoid(gate)
    act = gate * sig
    out[:, :FW] = (act * up).astype(BF)
    out[:, FW : 2 * FW] = (grad * up * sig * (1.0 + gate * (1.0 - sig))).astype(BF)
    out[:, 2 * FW :] = (grad * act).astype(BF)


def rows_kernel(*refs):
    hs, ws, outs = refs[:4], refs[4], refs[5:]
    rows = hs[0].shape[0]
    hidden, ggate, gup = thirds(hs)
    for a in range(SIDE):
        cols = slice(a * COLS, a * COLS + COLS)
        made = dot_last(hidden, ws[a, 2]).astype(BF)
        back = (dot_last(ggate, ws[a, 0]) + dot_last(gup, ws[a, 1])).astype(BF)
        for p in range(SIDE):
            outs[p][0, :, cols] = made[p * rows : p * rows + rows]
            outs[p][1, :, cols] = back[p * rows : p * rows + rows]


def weights_kernel(*refs):
    hs, xs, out = refs[:8], refs[8:16], refs[16]
    hidden, ggate, gup = thirds(hs)
    for a in range(SIDE):
        cols = slice(a * COLS, a * COLS + COLS)
        x, g = stacked(xs, 0, cols), stacked(xs, 1, cols)
        for k, (left, right) in enumerate(((x, ggate), (x, gup), (g, hidden))):
            out[a, k] = dot_first(left, right).astype(BF)


def total_kernel(summed, *outs):
    for k in range(3):
        outs[k][0] = summed[k].astype(F32)


def combine_kernel(place, ids, gates, cotangent, *refs):
    backs, (mixed, gtok, ggates) = refs[:REL], refs[REL:]
    labels, chosen, scale = routing(place, ids[...], gates[...])
    spread = chosen.T.astype(BF)
    scores = jnp.zeros(chosen.shape, F32)
    for blk in range(16):
        cols = slice(blk * COLS, blk * COLS + COLS)
        made, grads = [], []
        for dc in range(2):
            sb, sa = block_place(place, dc, blk // 4, blk % 4)
            lanes = pl.ds(pl.multiple_of(sa * COLS, COLS), COLS)
            for dz in range(4):
                made.append(backs[dc * 4 + dz][0, sb, :, lanes])
                grads.append(backs[dc * 4 + dz][1, sb, :, lanes])
        made, grads = jnp.concatenate(made, axis=0), jnp.concatenate(grads, axis=0)
        scaled = scale * made.astype(F32)
        upper = scaled.astype(BF)
        lower = (scaled - upper.astype(F32)).astype(BF)
        mixed[:, cols] = (dot(spread, upper) + dot(spread, lower)).astype(BF)
        gtok[:, cols] = dot(spread, grads).astype(BF)
        scores += dot_last(made, cotangent[:, cols])
    picked = chosen * scores
    total = jnp.zeros(ids.shape, F32)
    for r in range(REL):
        mine = jnp.sum(picked[r * CAP : r * CAP + CAP], axis=0, keepdims=True)
        total += jnp.where(ids[...] == labels[r], mine, 0.0)
    ggates[...] = total


def per_device(tokens, expert_ids, gates, cotangent, w_gate, w_up, w_down):
    tok, width = tokens.shape
    dp, ex = lax.axis_index("dp"), lax.axis_index("expert")
    place = jnp.stack([dp // 4, dp % 4, ex // 2, ex % 2]).astype(jnp.int32)
    ids_t, gates_t = expert_ids.T, gates.T
    chunk = width // SIDE
    rows = SIDE * CAP
    work = 2 * SIDE * rows * chunk * 3 * FW

    (held,) = call(
        held_kernel,
        [shape((3, COLS, FW))],
        (w_gate, w_up, w_down),
        0,
        hbm=3,
        vmem=60 * 2**20,
        scratch=[pltpu.SemaphoreType.DMA((3,))],
    )
    ws = lax.all_gather(held, AXES, axis_index_groups=groups_a())

    sends = call(
        dispatch_kernel,
        [shape((2, SIDE, CAP, chunk))] * REL,
        (place, ids_t, gates_t, tokens, cotangent),
        4 * tok * tok * width,
        smem=1,
        hbm=4,
        vmem=60 * 2**20,
        scratch=[
            pltpu.VMEM(ids_t.shape, jnp.int32),
            pltpu.VMEM(ids_t.shape, F32),
            pltpu.VMEM((SIDE, tok, chunk), BF),
            pltpu.VMEM((SIDE, tok, chunk), BF),
            pltpu.SemaphoreType.DMA((10,)),
        ],
    )
    came = [sends[0]] + [shift_z(sends[r], r % 4, r // 4) for r in range(1, REL)]
    xs, hs, backs = [], [], []
    for half in range(2):
        turned = call(
            to_b_kernel,
            [shape((2, rows, chunk))] * SIDE,
            came[half * SIDE : half * SIDE + SIDE],
            0,
        )
        xs.append([turned[0]] + [shift_b(turned[s], s) for s in (1, 2, 3)])
    blocks = [shape((rows, 3 * FW), F32)] + [shape((rows, 3 * FW))] * 3
    parts = call(partial_kernel, blocks * 2, (*xs[0], *xs[1], ws), 2 * work)
    for half in range(2):
        own, *sent = parts[half * SIDE : half * SIDE + SIDE]
        others = [shift_b(sent[s - 1], -s) for s in (1, 2, 3)]
        (mid,) = call(hidden_kernel, [shape((rows, 3 * FW))], (own, *others), 0)
        hs.append([mid] + [shift_b(mid, s) for s in (1, 2, 3)])

    def send_back(half, hs):
        outs = call(
            rows_kernel, [shape((2, rows, chunk))] * SIDE, (*hs, ws), work
        )
        return [outs[0]] + [shift_b(outs[s], -s) for s in (1, 2, 3)], outs

    def to_source(half, home):
        split = call(to_z_kernel, [shape((2, SIDE, CAP, chunk))] * SIDE, home, 0)
        return [split[dz] if dz + half == 0 else shift_z(split[dz], -dz, half) for dz in range(SIDE)]

    home_a, _ = send_back(0, hs[0])
    hs_b, _ = lax.optimization_barrier((hs[1], (home_a[1], home_a[3])))
    (grads,) = call(
        weights_kernel,
        [shape((SIDE, 3, COLS, FW))],
        (*hs[0], *hs_b, *xs[0], *xs[1]),
        2 * work,
    )
    home_b, _ = send_back(1, lax.optimization_barrier((hs[1], grads))[0])
    total = lax.psum_scatter(grads, AXES, axis_index_groups=groups_a())
    backs = to_source(0, home_a) + to_source(1, home_b)
    gw = call(total_kernel, [shape((1, COLS, FW), F32)] * 3, (total,), 0)
    backs, gw = lax.optimization_barrier((backs, gw))
    mixed, gtok, gg_t = call(
        combine_kernel,
        [shape((tok, width)), shape((tok, width)), shape(ids_t.shape, F32)],
        (place, ids_t, gates_t, cotangent, *backs),
        8 * tok * tok * width,
        smem=1,
    )
    return mixed, gtok, gg_t.T, *gw


def solution(mesh):
    rows, cut = P(("dp", "expert"), None), P("expert", "dp", None)
    return jax.shard_map(
        per_device,
        mesh=mesh,
        in_specs=(rows,) * 4 + (cut,) * 3,
        out_specs=(rows,) * 3 + (cut,) * 3,
        check_vma=False,
    )
```

```python
import functools

import jax
import jax.numpy as jnp
from jax import lax
from jax.experimental import pallas as pl
from jax.experimental.pallas import tpu as pltpu
from jax.sharding import PartitionSpec as P

CAP = 16
SIDE = 4
AXES = ("dp", "expert")
BF = jnp.bfloat16
F32 = jnp.float32
REL = 8
COLS = 256
FW = 768
VMEM = 12 * 2**20


def _dev(y, x, z, c):
    return ((y % SIDE) * SIDE + x % SIDE) * 8 + (z % SIDE) * 2 + c % 2


def _perm(move):
    pairs = []
    for i in range(128):
        y, x, z, c = i // 32, i // 8 % 4, i // 2 % 4, i % 2
        pairs.append((i, _dev(*move(y, x, z, c))))
    return pairs


def groups_a():
    groups = [[_dev(y, x, z, 0) for x in range(4)] for y in range(4) for z in range(4)]
    return groups + [[_dev(y, x, z, 1) for y in range(4)] for x in range(4) for z in range(4)]


def shift_b(v, s):
    return lax.ppermute(
        v, AXES, _perm(lambda y, x, z, c: (y + s, x, z, c) if c == 0 else (y, x + s, z, c))
    )


def shift_z(v, dz, dc):
    return lax.ppermute(v, AXES, _perm(lambda y, x, z, c: (y, x, z + dz, c + dc)))


def dot(left, right):
    return jnp.dot(left, right, preferred_element_type=F32)


def dot_last(left, right):
    return lax.dot_general(left, right, (((1,), (1,)), ((), ())), preferred_element_type=F32)


def dot_first(left, right):
    return lax.dot_general(left, right, (((0,), (0,)), ((), ())), preferred_element_type=F32)


def call(kernel, outs, ins, flops, smem=0, hbm=0, scratch=(), vmem=VMEM):
    spaces = [pltpu.SMEM] * smem + [pltpu.HBM] * hbm + [pltpu.VMEM] * (len(ins) - smem - hbm)
    return pl.pallas_call(
        kernel,
        out_shape=tuple(outs),
        in_specs=[pl.BlockSpec(memory_space=space) for space in spaces],
        out_specs=tuple(pl.BlockSpec(memory_space=pltpu.VMEM) for _ in outs),
        scratch_shapes=list(scratch),
        compiler_params=pltpu.CompilerParams(vmem_limit_bytes=vmem),
        cost_estimate=pl.CostEstimate(flops=flops // 100, bytes_accessed=1024, transcendentals=0),
    )(*ins)


def shape(dims, dtype=BF):
    return jax.ShapeDtypeStruct(dims, dtype)


def routing(place, ids, gates):
    tok = ids.shape[1]
    z, c = place[2], place[3]
    labels, used, weight = [], [], []
    for r in range(REL):
        label = ((z + r % 4) & 3) * 2 + (c ^ (r // 4))
        hit = ids == label
        labels.append(label)
        used.append(jnp.sum(jnp.where(hit, 1.0, 0.0), axis=0, keepdims=True))
        weight.append(jnp.sum(jnp.where(hit, gates, 0.0), axis=0, keepdims=True))
    used_all = jnp.concatenate(used, axis=0)
    before = lax.broadcasted_iota(jnp.int32, (tok, tok), 0) < lax.broadcasted_iota(
        jnp.int32, (tok, tok), 1
    )
    position = dot(used_all.astype(BF), jnp.where(before, 1.0, 0.0).astype(BF))
    slot = lax.broadcasted_iota(jnp.int32, (CAP, tok), 0).astype(F32)
    chosen, scale = [], []
    for r in range(REL):
        mask = (position[r : r + 1] == slot) & (used[r] > 0.5)
        chosen.append(jnp.where(mask, 1.0, 0.0))
        scale.append(jnp.sum(jnp.where(mask, weight[r], 0.0), axis=1, keepdims=True))
    return labels, jnp.concatenate(chosen, axis=0), jnp.concatenate(scale, axis=0)


def block_place(place, dc, yb, xb):
    y, x, c = place[0], place[1], place[3]
    dy, dx = (yb - y + 4) & 3, (xb - x + 4) & 3
    flip = c ^ dc
    return jnp.where(flip == 0, dy, dx), jnp.where(flip == 0, xb, yb)


def dispatch_kernel(place, ids, gates, tokens, cotangent, *refs):
    outs, (ids_v, gates_v, tok_v, cot_v, sem) = refs[:REL], refs[REL:]
    small = [
        pltpu.make_async_copy(ids, ids_v, sem.at[0]),
        pltpu.make_async_copy(gates, gates_v, sem.at[1]),
    ]
    part = tokens.shape[0] // SIDE
    wide = []
    for k, (src, dst) in enumerate(((tokens, tok_v), (cotangent, cot_v))):
        for q in range(SIDE):
            at = pl.ds(q * part, part)
            wide.append(pltpu.make_async_copy(src.at[at], dst.at[at], sem.at[2 + SIDE * k + q]))
    for copy in small + wide:
        copy.start()
    for copy in small:
        copy.wait()
    _, chosen, scale = routing(place, ids_v[...], gates_v[...])
    chosen = chosen.astype(BF)
    for kind, held in enumerate((tok_v, cot_v)):
        for copy in wide[SIDE * kind : SIDE * kind + SIDE]:
            copy.wait()
        for blk in range(16):
            rows = dot(chosen, held[:, blk * COLS : blk * COLS + COLS])
            rows = (scale * rows if kind else rows).astype(BF)
            for dc in range(2):
                sb, sa = block_place(place, dc, blk // 4, blk % 4)
                lanes = pl.ds(pl.multiple_of(sa * COLS, COLS), COLS)
                for dz in range(4):
                    r = dc * 4 + dz
                    outs[r][kind, sb, :, lanes] = rows[r * CAP : r * CAP + CAP]


def to_b_kernel(*refs):
    ins, outs = refs[:SIDE], refs[SIDE:]
    for s in range(SIDE):
        for r in range(SIDE):
            for kind in range(2):
                outs[s][kind, r * CAP : r * CAP + CAP, :] = ins[r][kind, s]


def to_z_kernel(*refs):
    ins, outs = refs[:SIDE], refs[SIDE:]
    for s in range(SIDE):
        for r in range(SIDE):
            for kind in range(2):
                outs[r][kind, s] = ins[s][kind, r * CAP : r * CAP + CAP, :]


def stacked(pieces, kind, cols=slice(None)):
    return jnp.concatenate([p[kind, :, cols] for p in pieces], axis=0)


def thirds(pieces):
    return [jnp.concatenate([p[:, k * FW : k * FW + FW] for p in pieces], axis=0) for k in range(3)]


def held_kernel(gate, up, down, out, sem):
    copies = [
        pltpu.make_async_copy(w.at[0], out.at[k], sem.at[k]) for k, w in enumerate((gate, up, down))
    ]
    for copy in copies:
        copy.start()
    for copy in copies:
        copy.wait()


def partial_kernel(*refs):
    xs, ws, outs = refs[:8], refs[8], refs[9:]
    rows = xs[0].shape[1]
    for which in range(3):
        left = stacked(xs, 0 if which < 2 else 1)
        for n in range(FW // COLS):
            cols = slice(n * COLS, n * COLS + COLS)
            at = slice(which * FW + n * COLS, which * FW + n * COLS + COLS)
            right = jnp.concatenate([ws[a, which, :, cols] for a in range(SIDE)], axis=0)
            got = dot(left, right)
            for p in range(2 * SIDE):
                outs[p][:, at] = got[p * rows : p * rows + rows].astype(outs[p].dtype)


def hidden_kernel(own, p1, p2, p3, out):
    def full(which):
        at = slice(which * FW, which * FW + FW)
        return (own[:, at] + p1[:, at].astype(F32)) + (
            p2[:, at].astype(F32) + p3[:, at].astype(F32)
        )

    gate, up, grad = full(0), full(1), full(2)
    sig = jax.nn.sigmoid(gate)
    act = gate * sig
    out[:, :FW] = (act * up).astype(BF)
    out[:, FW : 2 * FW] = (grad * up * sig * (1.0 + gate * (1.0 - sig))).astype(BF)
    out[:, 2 * FW :] = (grad * act).astype(BF)


def rows_kernel(*refs):
    hs, ws, outs = refs[:4], refs[4], refs[5:]
    rows = hs[0].shape[0]
    hidden, ggate, gup = thirds(hs)
    for a in range(SIDE):
        cols = slice(a * COLS, a * COLS + COLS)
        made = dot_last(hidden, ws[a, 2]).astype(BF)
        back = (dot_last(ggate, ws[a, 0]) + dot_last(gup, ws[a, 1])).astype(BF)
        for p in range(SIDE):
            outs[p][0, :, cols] = made[p * rows : p * rows + rows]
            outs[p][1, :, cols] = back[p * rows : p * rows + rows]


def weights_kernel(*refs):
    hs, xs, out = refs[:8], refs[8:16], refs[16]
    hidden, ggate, gup = thirds(hs)
    for a in range(SIDE):
        cols = slice(a * COLS, a * COLS + COLS)
        x, g = stacked(xs, 0, cols), stacked(xs, 1, cols)
        for k, (left, right) in enumerate(((x, ggate), (x, gup), (g, hidden))):
            out[a, k] = dot_first(left, right).astype(BF)


def total_kernel(summed, *outs):
    for k in range(3):
        outs[k][0] = summed[k].astype(F32)


def combine_kernel(half, place, ids, gates, cotangent, *refs):
    backs, (mixed, gtok, ggates) = refs[:SIDE], refs[-3:]
    held = refs[SIDE:-3]
    labels, chosen, scale = routing(place, ids[...], gates[...])
    slots = slice(half * SIDE * CAP, half * SIDE * CAP + SIDE * CAP)
    labels, chosen, scale = labels[half * SIDE :][:SIDE], chosen[slots], scale[slots]
    spread = chosen.T.astype(BF)
    scores = jnp.zeros(chosen.shape, F32)
    for blk in range(16):
        cols = slice(blk * COLS, blk * COLS + COLS)
        sb, sa = block_place(place, half, blk // 4, blk % 4)
        lanes = pl.ds(pl.multiple_of(sa * COLS, COLS), COLS)
        made, grads = (
            jnp.concatenate([b[kind, sb, :, lanes] for b in backs], axis=0) for kind in range(2)
        )
        scaled = scale * made.astype(F32)
        upper = scaled.astype(BF)
        lower = (scaled - upper.astype(F32)).astype(BF)
        mix, gto = dot(spread, upper) + dot(spread, lower), dot(spread, grads)
        if held:
            mix, gto = mix + held[0][:, cols], gto + held[1][:, cols]
        mixed[:, cols] = mix.astype(mixed.dtype)
        gtok[:, cols] = gto.astype(gtok.dtype)
        scores += dot_last(made, cotangent[:, cols])
    picked = chosen * scores
    total = held[2][...] if held else jnp.zeros(ids.shape, F32)
    for r in range(SIDE):
        mine = jnp.sum(picked[r * CAP : r * CAP + CAP], axis=0, keepdims=True)
        total += jnp.where(ids[...] == labels[r], mine, 0.0)
    ggates[...] = total


def per_device(tokens, expert_ids, gates, cotangent, w_gate, w_up, w_down):
    tok, width = tokens.shape
    dp, ex = lax.axis_index("dp"), lax.axis_index("expert")
    place = jnp.stack([dp // 4, dp % 4, ex // 2, ex % 2]).astype(jnp.int32)
    ids_t, gates_t = expert_ids.T, gates.T
    chunk = width // SIDE
    rows = SIDE * CAP
    work = 2 * SIDE * rows * chunk * 3 * FW

    (held,) = call(
        held_kernel,
        [shape((3, COLS, FW))],
        (w_gate, w_up, w_down),
        0,
        hbm=3,
        vmem=60 * 2**20,
        scratch=[pltpu.SemaphoreType.DMA((3,))],
    )
    ws = lax.all_gather(held, AXES, axis_index_groups=groups_a())

    sends = call(
        dispatch_kernel,
        [shape((2, SIDE, CAP, chunk))] * REL,
        (place, ids_t, gates_t, tokens, cotangent),
        4 * tok * tok * width,
        smem=1,
        hbm=4,
        vmem=60 * 2**20,
        scratch=[
            pltpu.VMEM(ids_t.shape, jnp.int32),
            pltpu.VMEM(ids_t.shape, F32),
            pltpu.VMEM(tokens.shape, BF),
            pltpu.VMEM(tokens.shape, BF),
            pltpu.SemaphoreType.DMA((10,)),
        ],
    )
    came = [sends[0]] + [shift_z(sends[r], r % 4, r // 4) for r in range(1, REL)]
    xs, hs, backs = [], [], []
    for half in range(2):
        turned = call(
            to_b_kernel,
            [shape((2, rows, chunk))] * SIDE,
            came[half * SIDE : half * SIDE + SIDE],
            0,
        )
        xs.append([turned[0]] + [shift_b(turned[s], s) for s in (1, 2, 3)])
    blocks = [shape((rows, 3 * FW), F32)] + [shape((rows, 3 * FW))] * 3
    parts = call(partial_kernel, blocks * 2, (*xs[0], *xs[1], ws), 2 * work)
    for half in range(2):
        own, *sent = parts[half * SIDE : half * SIDE + SIDE]
        others = [shift_b(sent[s - 1], -s) for s in (1, 2, 3)]
        (mid,) = call(hidden_kernel, [shape((rows, 3 * FW))], (own, *others), 0)
        hs.append([mid] + [shift_b(mid, s) for s in (1, 2, 3)])

    def send_back(half, hs):
        outs = call(
            rows_kernel, [shape((2, rows, chunk))] * SIDE, (*hs, ws), work
        )
        return [outs[0]] + [shift_b(outs[s], -s) for s in (1, 2, 3)], outs

    def to_source(half, home):
        split = call(to_z_kernel, [shape((2, SIDE, CAP, chunk))] * SIDE, home, 0)
        sent = [split[dz] if dz + half == 0 else shift_z(split[dz], -dz, half) for dz in range(SIDE)]
        return sent, split

    home_a, outs = send_back(0, hs[0])
    home_b, outs = send_back(1, lax.optimization_barrier((hs[1], outs[0]))[0])
    backs, split = to_source(0, lax.optimization_barrier((home_a, outs[0]))[0])
    hs_b, _ = lax.optimization_barrier((hs[1], (outs[0], split[0])))
    (grads,) = call(
        weights_kernel,
        [shape((SIDE, 3, COLS, FW))],
        (*hs[0], *hs_b, *xs[0], *xs[1]),
        2 * work,
    )
    total = lax.psum_scatter(grads, AXES, axis_index_groups=groups_a())
    late, _ = to_source(1, lax.optimization_barrier((home_b, (grads, split[0])))[0])

    def combine(half, dtype, ins):
        return call(
            functools.partial(combine_kernel, half),
            [shape((tok, width), dtype), shape((tok, width), dtype), shape(ids_t.shape, F32)],
            (place, ids_t, gates_t, cotangent, *ins),
            4 * tok * tok * width,
            smem=1,
        )

    sums = combine(0, F32, backs)
    mixed, gtok, gg_t = combine(1, BF, (*late, *sums))
    total, _ = lax.optimization_barrier((total, gg_t))
    gw = call(total_kernel, [shape((1, COLS, FW), F32)] * 3, (total,), 0)
    return mixed, gtok, gg_t.T, *gw


def solution(mesh):
    rows, cut = P(("dp", "expert"), None), P("expert", "dp", None)
    return jax.shard_map(
        per_device,
        mesh=mesh,
        in_specs=(rows,) * 4 + (cut,) * 3,
        out_specs=(rows,) * 3 + (cut,) * 3,
        check_vma=False,
    )
```

```python
import functools

import jax
import jax.numpy as jnp
from jax import lax
from jax.experimental import pallas as pl
from jax.experimental.pallas import tpu as pltpu
from jax.sharding import PartitionSpec as P

CAP = 16
SIDE = 4
AXES = ("dp", "expert")
BF = jnp.bfloat16
F32 = jnp.float32
REL = 8
COLS = 256
FW = 768
VMEM = 12 * 2**20


def _dev(y, x, z, c):
    return ((y % SIDE) * SIDE + x % SIDE) * 8 + (z % SIDE) * 2 + c % 2


def _perm(move):
    pairs = []
    for i in range(128):
        y, x, z, c = i // 32, i // 8 % 4, i // 2 % 4, i % 2
        pairs.append((i, _dev(*move(y, x, z, c))))
    return pairs


def groups_a():
    groups = [[_dev(y, x, z, 0) for x in range(4)] for y in range(4) for z in range(4)]
    return groups + [[_dev(y, x, z, 1) for y in range(4)] for x in range(4) for z in range(4)]


def shift_b(v, s):
    return lax.ppermute(
        v, AXES, _perm(lambda y, x, z, c: (y + s, x, z, c) if c == 0 else (y, x + s, z, c))
    )


def shift_z(v, dz, dc):
    return lax.ppermute(v, AXES, _perm(lambda y, x, z, c: (y, x, z + dz, c + dc)))


def dot(left, right):
    return jnp.dot(left, right, preferred_element_type=F32)


def dot_last(left, right):
    return lax.dot_general(left, right, (((1,), (1,)), ((), ())), preferred_element_type=F32)


def dot_first(left, right):
    return lax.dot_general(left, right, (((0,), (0,)), ((), ())), preferred_element_type=F32)


def call(kernel, outs, ins, flops, smem=0, hbm=0, scratch=(), vmem=VMEM, out_space=pltpu.VMEM):
    spaces = [pltpu.SMEM] * smem + [pltpu.HBM] * hbm + [pltpu.VMEM] * (len(ins) - smem - hbm)
    return pl.pallas_call(
        kernel,
        out_shape=tuple(outs),
        in_specs=[pl.BlockSpec(memory_space=space) for space in spaces],
        out_specs=tuple(pl.BlockSpec(memory_space=out_space) for _ in outs),
        scratch_shapes=list(scratch),
        compiler_params=pltpu.CompilerParams(vmem_limit_bytes=vmem),
        cost_estimate=pl.CostEstimate(flops=flops // 100, bytes_accessed=1024, transcendentals=0),
    )(*ins)


def shape(dims, dtype=BF):
    return jax.ShapeDtypeStruct(dims, dtype)


def routing(place, ids, gates):
    tok = ids.shape[1]
    z, c = place[2], place[3]
    labels, used, weight = [], [], []
    for r in range(REL):
        label = ((z + r % 4) & 3) * 2 + (c ^ (r // 4))
        hit = ids == label
        labels.append(label)
        used.append(jnp.sum(jnp.where(hit, 1.0, 0.0), axis=0, keepdims=True))
        weight.append(jnp.sum(jnp.where(hit, gates, 0.0), axis=0, keepdims=True))
    used_all = jnp.concatenate(used, axis=0)
    before = lax.broadcasted_iota(jnp.int32, (tok, tok), 0) < lax.broadcasted_iota(
        jnp.int32, (tok, tok), 1
    )
    position = dot(used_all.astype(BF), jnp.where(before, 1.0, 0.0).astype(BF))
    slot = lax.broadcasted_iota(jnp.int32, (CAP, tok), 0).astype(F32)
    chosen, scale = [], []
    for r in range(REL):
        mask = (position[r : r + 1] == slot) & (used[r] > 0.5)
        chosen.append(jnp.where(mask, 1.0, 0.0))
        scale.append(jnp.sum(jnp.where(mask, weight[r], 0.0), axis=1, keepdims=True))
    return labels, jnp.concatenate(chosen, axis=0), jnp.concatenate(scale, axis=0)


def block_place(place, dc, yb, xb):
    y, x, c = place[0], place[1], place[3]
    dy, dx = (yb - y + 4) & 3, (xb - x + 4) & 3
    flip = c ^ dc
    return jnp.where(flip == 0, dy, dx), jnp.where(flip == 0, xb, yb)


def dispatch_kernel(place, ids, gates, tokens, cotangent, *refs):
    outs, (ids_v, gates_v, tok_v, cot_v, sem) = refs[:REL], refs[REL:]
    small = [
        pltpu.make_async_copy(ids, ids_v, sem.at[0]),
        pltpu.make_async_copy(gates, gates_v, sem.at[1]),
    ]
    part = tokens.shape[0] // SIDE
    wide = []
    for k, (src, dst) in enumerate(((tokens, tok_v), (cotangent, cot_v))):
        for q in range(SIDE):
            at = pl.ds(q * part, part)
            wide.append(pltpu.make_async_copy(src.at[at], dst.at[at], sem.at[2 + SIDE * k + q]))
    for copy in small + wide:
        copy.start()
    for copy in small:
        copy.wait()
    _, chosen, scale = routing(place, ids_v[...], gates_v[...])
    chosen = chosen.astype(BF)
    for kind, held in enumerate((tok_v, cot_v)):
        for copy in wide[SIDE * kind : SIDE * kind + SIDE]:
            copy.wait()
        for blk in range(16):
            rows = dot(chosen, held[:, blk * COLS : blk * COLS + COLS])
            rows = (scale * rows if kind else rows).astype(BF)
            for dc in range(2):
                sb, sa = block_place(place, dc, blk // 4, blk % 4)
                lanes = pl.ds(pl.multiple_of(sa * COLS, COLS), COLS)
                for dz in range(4):
                    r = dc * 4 + dz
                    outs[r][kind, sb, :, lanes] = rows[r * CAP : r * CAP + CAP]


def to_b_kernel(*refs):
    ins, outs = refs[:SIDE], refs[SIDE:]
    for s in range(SIDE):
        for r in range(SIDE):
            for kind in range(2):
                outs[s][kind, r * CAP : r * CAP + CAP, :] = ins[r][kind, s]


def to_z_kernel(*refs):
    ins, outs = refs[:SIDE], refs[SIDE:]
    for s in range(SIDE):
        for r in range(SIDE):
            for kind in range(2):
                outs[r][kind, s] = ins[s][kind, r * CAP : r * CAP + CAP, :]


def stacked(pieces, kind, cols=slice(None)):
    return jnp.concatenate([p[kind, :, cols] for p in pieces], axis=0)


def thirds(pieces):
    return [jnp.concatenate([p[:, k * FW : k * FW + FW] for p in pieces], axis=0) for k in range(3)]


def held_kernel(gate, up, down, out, block, sem):
    half = COLS // 2
    steps = []
    for k, w in enumerate((gate, up, down)):
        for h in range(2):
            at = pl.ds(h * half, half)
            took, gave = sem.at[0, 2 * k + h], sem.at[1, 2 * k + h]
            steps.append(
                (
                    pltpu.make_async_copy(w.at[0, at], block.at[k, at], took),
                    pltpu.make_async_copy(block.at[k, at], out.at[k, at], gave),
                )
            )
    for take, _ in steps:
        take.start()
    for take, give in steps:
        take.wait()
        give.start()
    for _, give in steps:
        give.wait()


def partial_kernel(*refs):
    xs, ws, outs = refs[:8], refs[8], refs[9:]
    rows = xs[0].shape[1]
    for which in range(3):
        left = stacked(xs, 0 if which < 2 else 1)
        for n in range(FW // COLS):
            cols = slice(n * COLS, n * COLS + COLS)
            at = slice(which * FW + n * COLS, which * FW + n * COLS + COLS)
            right = jnp.concatenate([ws[a, which, :, cols] for a in range(SIDE)], axis=0)
            got = dot(left, right)
            for p in range(2 * SIDE):
                outs[p][:, at] = got[p * rows : p * rows + rows].astype(outs[p].dtype)


def hidden_kernel(own, p1, p2, p3, out):
    def full(which):
        at = slice(which * FW, which * FW + FW)
        return (own[:, at] + p1[:, at].astype(F32)) + (
            p2[:, at].astype(F32) + p3[:, at].astype(F32)
        )

    gate, up, grad = full(0), full(1), full(2)
    sig = jax.nn.sigmoid(gate)
    act = gate * sig
    out[:, :FW] = (act * up).astype(BF)
    out[:, FW : 2 * FW] = (grad * up * sig * (1.0 + gate * (1.0 - sig))).astype(BF)
    out[:, 2 * FW :] = (grad * act).astype(BF)


def rows_kernel(*refs):
    hs, ws, outs = refs[:4], refs[4], refs[5:]
    rows = hs[0].shape[0]
    hidden, ggate, gup = thirds(hs)
    for a in range(SIDE):
        cols = slice(a * COLS, a * COLS + COLS)
        made = dot_last(hidden, ws[a, 2]).astype(BF)
        back = (dot_last(ggate, ws[a, 0]) + dot_last(gup, ws[a, 1])).astype(BF)
        for p in range(SIDE):
            outs[p][0, :, cols] = made[p * rows : p * rows + rows]
            outs[p][1, :, cols] = back[p * rows : p * rows + rows]


def weights_kernel(*refs):
    hs, xs, out = refs[:8], refs[8:16], refs[16]
    hidden, ggate, gup = thirds(hs)
    for a in range(SIDE):
        cols = slice(a * COLS, a * COLS + COLS)
        x, g = stacked(xs, 0, cols), stacked(xs, 1, cols)
        for k, (left, right) in enumerate(((x, ggate), (x, gup), (g, hidden))):
            out[a, k] = dot_first(left, right).astype(BF)


def total_kernel(summed, *refs):
    outs, (narrow, wide, sem) = refs[:3], refs[3:]
    takes = [pltpu.make_async_copy(summed.at[k], narrow.at[k], sem.at[0, k]) for k in range(3)]
    gives = [pltpu.make_async_copy(wide.at[k], outs[k].at[0], sem.at[1, k]) for k in range(3)]
    for copy in takes:
        copy.start()
    for k in range(3):
        takes[k].wait()
        wide[k] = narrow[k].astype(F32)
        gives[k].start()
    for copy in gives:
        copy.wait()


def combine_kernel(half, place, ids, gates, cotangent, *refs):
    backs, (mixed, gtok, ggates) = refs[:SIDE], refs[-3:]
    held = refs[SIDE:-3]
    labels, chosen, scale = routing(place, ids[...], gates[...])
    slots = slice(half * SIDE * CAP, half * SIDE * CAP + SIDE * CAP)
    labels, chosen, scale = labels[half * SIDE :][:SIDE], chosen[slots], scale[slots]
    spread = chosen.T.astype(BF)
    scores = jnp.zeros(chosen.shape, F32)
    twice = jnp.concatenate([spread, spread], axis=1)
    y, x, flip = place[0], place[1], place[3] ^ half
    for sb in range(SIDE):
        made, grads = (jnp.concatenate([b[kind, sb] for b in backs], axis=0) for kind in range(2))
        scaled = scale * made.astype(F32)
        upper = scaled.astype(BF)
        lower = (scaled - upper.astype(F32)).astype(BF)
        mix, gto = dot(twice, jnp.concatenate([upper, lower], axis=0)), dot(spread, grads)
        given = []
        for sa in range(SIDE):
            blk = jnp.where(flip == 0, ((y + sb) & 3) * SIDE + sa, sa * SIDE + ((x + sb) & 3))
            cols = pl.ds(pl.multiple_of(blk * COLS, COLS), COLS)
            part = slice(sa * COLS, sa * COLS + COLS)
            one, two = mix[:, part], gto[:, part]
            if held:
                one, two = one + held[0][:, cols], two + held[1][:, cols]
            mixed[:, cols] = one.astype(mixed.dtype)
            gtok[:, cols] = two.astype(gtok.dtype)
            given.append(cotangent[:, cols])
        scores += dot_last(made, jnp.concatenate(given, axis=1))
    picked = chosen * scores
    total = held[2][...] if held else jnp.zeros(ids.shape, F32)
    for r in range(SIDE):
        mine = jnp.sum(picked[r * CAP : r * CAP + CAP], axis=0, keepdims=True)
        total += jnp.where(ids[...] == labels[r], mine, 0.0)
    ggates[...] = total


def per_device(tokens, expert_ids, gates, cotangent, w_gate, w_up, w_down):
    tok, width = tokens.shape
    dp, ex = lax.axis_index("dp"), lax.axis_index("expert")
    place = jnp.stack([dp // 4, dp % 4, ex // 2, ex % 2]).astype(jnp.int32)
    ids_t, gates_t = expert_ids.T, gates.T
    chunk = width // SIDE
    rows = SIDE * CAP
    work = 2 * SIDE * rows * chunk * 3 * FW

    (held,) = call(
        held_kernel,
        [shape((3, COLS, FW))],
        (w_gate, w_up, w_down),
        0,
        hbm=3,
        vmem=60 * 2**20,
        scratch=[pltpu.VMEM((3, COLS, FW), BF), pltpu.SemaphoreType.DMA((2, 6))],
        out_space=pltpu.HBM,
    )
    ws = lax.all_gather(held, AXES, axis_index_groups=groups_a())

    sends = call(
        dispatch_kernel,
        [shape((2, SIDE, CAP, chunk))] * REL,
        (place, ids_t, gates_t, tokens, cotangent),
        4 * tok * tok * width,
        smem=1,
        hbm=4,
        vmem=60 * 2**20,
        scratch=[
            pltpu.VMEM(ids_t.shape, jnp.int32),
            pltpu.VMEM(ids_t.shape, F32),
            pltpu.VMEM(tokens.shape, BF),
            pltpu.VMEM(tokens.shape, BF),
            pltpu.SemaphoreType.DMA((10,)),
        ],
    )
    came = [sends[0]] + [shift_z(sends[r], r % 4, r // 4) for r in range(1, REL)]
    xs, hs, backs = [], [], []
    for half in range(2):
        turned = call(
            to_b_kernel,
            [shape((2, rows, chunk))] * SIDE,
            came[half * SIDE : half * SIDE + SIDE],
            0,
        )
        xs.append([turned[0]] + [shift_b(turned[s], s) for s in (1, 2, 3)])
    blocks = [shape((rows, 3 * FW), F32)] + [shape((rows, 3 * FW))] * 3
    parts = call(partial_kernel, blocks * 2, (*xs[0], *xs[1], ws), 2 * work)
    for half in range(2):
        own, *sent = parts[half * SIDE : half * SIDE + SIDE]
        others = [shift_b(sent[s - 1], -s) for s in (1, 2, 3)]
        (mid,) = call(hidden_kernel, [shape((rows, 3 * FW))], (own, *others), 0)
        hs.append([mid] + [shift_b(mid, s) for s in (1, 2, 3)])

    def send_back(half, hs):
        outs = call(
            rows_kernel, [shape((2, rows, chunk))] * SIDE, (*hs, ws), work
        )
        return [outs[0]] + [shift_b(outs[s], -s) for s in (1, 2, 3)], outs

    def to_source(half, home):
        split = call(to_z_kernel, [shape((2, SIDE, CAP, chunk))] * SIDE, home, 0)
        sent = [split[dz] if dz + half == 0 else shift_z(split[dz], -dz, half) for dz in range(SIDE)]
        return sent, split

    home_a, outs = send_back(0, hs[0])
    home_b, outs = send_back(1, lax.optimization_barrier((hs[1], outs[0]))[0])
    backs, split = to_source(0, lax.optimization_barrier((home_a, outs[0]))[0])
    hs_b, _ = lax.optimization_barrier((hs[1], (outs[0], split[0])))
    (grads,) = call(
        weights_kernel,
        [shape((SIDE, 3, COLS, FW))],
        (*hs[0], *hs_b, *xs[0], *xs[1]),
        2 * work,
    )
    total = lax.psum_scatter(grads, AXES, axis_index_groups=groups_a())
    late, _ = to_source(1, lax.optimization_barrier((home_b, (grads, split[0])))[0])

    def combine(half, dtype, ins):
        return call(
            functools.partial(combine_kernel, half),
            [shape((tok, width), dtype), shape((tok, width), dtype), shape(ids_t.shape, F32)],
            (place, ids_t, gates_t, cotangent, *ins),
            4 * tok * tok * width,
            smem=1,
        )

    sums = combine(0, F32, backs)
    mixed, gtok, gg_t = combine(1, BF, (*late, *sums))
    total, _ = lax.optimization_barrier((total, gg_t))
    gw = call(
        total_kernel,
        [shape((1, COLS, FW), F32)] * 3,
        (total,),
        0,
        hbm=1,
        scratch=[
            pltpu.VMEM((3, COLS, FW), BF),
            pltpu.VMEM((3, COLS, FW), F32),
            pltpu.SemaphoreType.DMA((2, 3)),
        ],
        vmem=60 * 2**20,
        out_space=pltpu.HBM,
    )
    return mixed, gtok, gg_t.T, *gw


def solution(mesh):
    rows, cut = P(("dp", "expert"), None), P("expert", "dp", None)
    return jax.shard_map(
        per_device,
        mesh=mesh,
        in_specs=(rows,) * 4 + (cut,) * 3,
        out_specs=(rows,) * 3 + (cut,) * 3,
        check_vma=False,
    )
```
